128 devices in a mesh: section: 16 (over z_lo, x, core), ha: 2 (over z_hi), wa: 4 (over y).
Axes of the slice: x: 4, y: 4, z: 4 (z_hi: 2, z_lo: 2; z = z_hi * 2 + z_lo), core: 2. Of those that a mesh axis runs over, the one named last changes fastest.
Arguments:
- queries: bfloat16 [16, 4, 4, 8, 16, 2560], P('section', None, 'ha', 'wa'), may hold values from -28 to 28
- keys_values: bfloat16 [2, 16, 4, 4, 8, 16, 2560], P(None, 'section', None, 'ha', 'wa'), may hold values from -28 to 28
- grad_out: bfloat16 [16, 4, 4, 8, 16, 2560], P('section', None, 'ha', 'wa'), may hold values from -6 to 6
- time_start: int32 [4, 4, 8], P(None, 'ha', 'wa'), may hold values from 0 to 1, as said below
Outputs:
- grad_qkv: bfloat16 [3, 16, 4, 4, 8, 16, 2560], P(None, 'section', None, 'ha', 'wa')
The draws below stay inside these ranges and needn't reach their ends.
Inputs may be any that keep to these rules, and one draw needn't show every extreme that they name: Each tile's window begins at most two tiles before the tile and never after it: max(0, t - 2) <= time_start[t, h, w] <= min(t, 1) for time index t.
All inputs are finite; a program needn't handle non-finite values.
Results may differ from the reference program's by a relative error of at most 0.012.
Values may be sent and summed in bfloat16 or wider, within the bound.
No kernel may reach another device: no remote copies, remote signals or barrier semaphores. Data moves between devices by JAX's collectives and lax.ppermute only.
A program may use at most 192 MiB of HBM per device.

```python
import jax
import jax.numpy as jnp
from jax import lax

HEADS = 20
HEAD_DIM = 128
GT = 4
HT = 2
WT = 2
SECTIONS = 16
GH = 4
GW = 8
TILE_TOK = 16
CHANNELS = 2560
N_HA = 2
N_WA = 4


def drawn_draw(key):
    base = jax.random.fold_in(key, 71)
    pair_shape = (2, SECTIONS, GT, GH, GW, TILE_TOK, CHANNELS)
    pairs = jnp.clip(jax.random.normal(jax.random.fold_in(base, 1), pair_shape, jnp.float32), -6.0, 6.0)
    queries = jnp.clip(jax.random.normal(jax.random.fold_in(base, 2), pair_shape[1:], jnp.float32), -6.0, 6.0)
    return (queries, pairs)


def draw_queries(key, part):
    return drawn_draw(key)[0].astype(jnp.bfloat16)


def draw_keys_values(key, part):
    return drawn_draw(key)[1].astype(jnp.bfloat16)


def draw_time_start(key, part):
    shifts = jax.random.randint(jax.random.fold_in(key, 5), (GT, GH, GW), 0, 3)
    tiles = jnp.arange(GT, dtype=jnp.int32)[:, None, None]
    return jnp.clip(tiles - shifts, 0, GT - 3).astype(jnp.int32)


def block_levels(own_key, shape, split, low, largest):
    factor_of = 1.0
    for axis_at, blocks in split:
        steps = jax.random.uniform(jax.random.fold_in(jax.random.fold_in(own_key, 6), axis_at), (blocks,), jnp.float32, low / len(split), largest / len(split))
        factor_of = factor_of * jnp.repeat(jnp.exp(steps), shape[axis_at] // blocks).reshape((-1,) + (1,) * (len(shape) - 1 - axis_at))
    return factor_of


def centred(stream_key, dims, deviation, limit, shards=(), held_as=jnp.bfloat16):
    loudness = block_levels(stream_key, dims, shards, -0.22, 0.18) if shards else 1.0
    array = jax.random.normal(stream_key, dims, jnp.float32) * deviation * loudness
    return jnp.minimum(jnp.maximum(array, -limit), limit).astype(held_as)


def setup_inputs(seed: int = 0) -> dict:
    splits = jax.random.split(jax.random.key(seed), 5)
    queries = draw_queries(jax.random.fold_in(splits[4], 71), 0)
    keys_values = draw_keys_values(jax.random.fold_in(splits[4], 71), 0)
    grad_out = centred(splits[2], (SECTIONS, GT, GH, GW, TILE_TOK, CHANNELS), 1.0, 6.0, ((0, 16), (2, 2), (3, 4)))
    time_start = draw_time_start(jax.random.fold_in(splits[4], 71), 0)
    return {"queries": queries, "keys_values": keys_values, "grad_out": grad_out, "time_start": time_start}


def tile_grads(query_block, pair_block, grad_block, starts, tile_tok):
    scale_factor = HEAD_DIM ** -0.5
    query_full = query_block.astype(jnp.float32)
    key_part = pair_block[0].astype(jnp.float32)
    value_part = pair_block[1].astype(jnp.float32)
    grad_full = grad_block.astype(jnp.float32)
    scores = jnp.einsum("qhd,khd->hqk", query_full, key_part) * scale_factor
    key_tile = jnp.arange(key_part.shape[0], dtype=jnp.int32) // (9 * tile_tok)
    window_low = jnp.repeat(starts.astype(jnp.int32), tile_tok)
    inside = (key_tile[None, :] >= window_low[:, None]) & (key_tile[None, :] < window_low[:, None] + 3)
    scores = jnp.where(inside[None], scores, -jnp.inf)
    maximum = jnp.max(scores, axis=-1, keepdims=True)
    weights = jnp.exp(scores - maximum)
    softmax_out = weights / jnp.sum(weights, axis=-1, keepdims=True)
    weights_low = softmax_out.astype(jnp.bfloat16).astype(jnp.float32)
    grad_probs = jnp.einsum("qhd,khd->hqk", grad_full, value_part)
    row_delta = jnp.sum(softmax_out * grad_probs, axis=-1, keepdims=True)
    grad_scores = (softmax_out * (grad_probs - row_delta)).astype(jnp.bfloat16).astype(jnp.float32)
    query_grad = jnp.einsum("hqk,khd->qhd", grad_scores, key_part) * scale_factor
    key_grad = jnp.einsum("hqk,qhd->khd", grad_scores, query_full) * scale_factor
    value_grad = jnp.einsum("hqk,qhd->khd", weights_low, grad_full)
    return query_grad, jnp.stack([key_grad, value_grad])


def reference(queries, keys_values, grad_out, time_start):
    tile_count = GT * TILE_TOK
    interior = jnp.zeros((HT + 2, WT + 2), dtype=bool).at[1:HT + 1, 1:WT + 1].set(True)

    def section_grads(operands):
        section_queries, section_pairs, section_grads_out = operands
        total = jnp.zeros((2, GT, GH + 2, GW + 2, TILE_TOK, CHANNELS), jnp.float32)
        query_total = jnp.zeros((GT, GH, GW, TILE_TOK, CHANNELS), jnp.bfloat16)
        for dev_row in range(N_HA):
            for dev_col in range(N_WA):
                partial_value = jnp.zeros((2, GT, HT + 2, WT + 2, TILE_TOK, CHANNELS), jnp.float32)
                for tile_row in range(HT):
                    for tile_col in range(WT):
                        glob_row = dev_row * HT + tile_row
                        glob_col = dev_col * WT + tile_col
                        top_start = min(max(glob_row - 1, 0), GH - 3)
                        left_start = min(max(glob_col - 1, 0), GW - 3)
                        window = section_pairs[:, :, top_start:top_start + 3, left_start:left_start + 3]
                        pair_block = window.reshape(2, tile_count * 9, HEADS, HEAD_DIM)
                        query_block = section_queries[:, glob_row, glob_col].reshape(tile_count, HEADS, HEAD_DIM)
                        grad_block = section_grads_out[:, glob_row, glob_col].reshape(tile_count, HEADS, HEAD_DIM)
                        query_grad, pair_grad = tile_grads(query_block, pair_block, grad_block, time_start[:, glob_row, glob_col], TILE_TOK)
                        query_total = query_total.at[:, glob_row, glob_col].set(query_grad.reshape(GT, TILE_TOK, CHANNELS).astype(jnp.bfloat16))
                        ext_row = top_start - dev_row * HT + 1
                        ext_col = left_start - dev_col * WT + 1
                        partial_value = partial_value.at[:, :, ext_row:ext_row + 3, ext_col:ext_col + 3].add(pair_grad.reshape(2, GT, 3, 3, TILE_TOK, CHANNELS))
                rim_values = lax.optimization_barrier(partial_value.astype(jnp.bfloat16)).astype(jnp.float32)
                mixed = jnp.where(interior[None, None, :, :, None, None], partial_value, rim_values)
                total = total.at[:, :, dev_row * HT:dev_row * HT + HT + 2, dev_col * WT:dev_col * WT + WT + 2].add(mixed)
        pair_total = total[:, :, 1:GH + 1, 1:GW + 1].astype(jnp.bfloat16)
        return jnp.concatenate([query_total[None], pair_total], axis=0)

    per_section = lax.map(section_grads, (queries, jnp.moveaxis(keys_values, 1, 0), grad_out))
    shifted = jnp.roll(per_section, -1, axis=0)
    return jnp.moveaxis(shifted, 0, 1)
```

```python
import functools

import jax
import jax.numpy as jnp
from jax import lax
from jax.experimental import pallas as pl
from jax.experimental.pallas import tpu as pltpu
from jax.sharding import PartitionSpec as P

HEAD_DIM = 128
SCALE = HEAD_DIM**-0.5
LOG2E = 1.4426950408889634
CHUNKS = (12, 8)
NEG = -1e30
GROUP = 2
BF = jnp.bfloat16
F32 = jnp.float32


def shift(block, axis, step):
    count = lax.axis_size(axis)
    return lax.ppermute(block, axis, [(i, (i + step) % count) for i in range(count)])


def shift_across(block):
    sections = lax.axis_size("section")
    route = []
    for i in range(sections):
        for h in range(2):
            route.append((i * 2 + h, (i - 1) % sections * 2 + 1 - h))
    return lax.ppermute(block, ("section", "ha"), route)


def nt(a, b):
    return lax.dot_general(a, b, (((1,), (1,)), ((), ())), preferred_element_type=F32)


def nn(a, b):
    return lax.dot_general(a, b, (((1,), (0,)), ((), ())), preferred_element_type=F32)


def tn(a, b):
    return lax.dot_general(a, b, (((0,), (0,)), ((), ())), preferred_element_type=F32)


def attend(
    base, place_ref, starts_ref, q_ref, g_ref, kv_ref, z_ref, xl_ref, xlc_ref, xr_ref, xrc_ref,
    dq_ref, own_ref, dz_ref, dxl_ref, dxlc_ref, dxr_ref, dxrc_ref,
):
    times = q_ref.shape[0]
    tok = q_ref.shape[3]
    heads = dq_ref.shape[4] // HEAD_DIM
    rows = times * 2 * tok
    n_kv, n_own, n_row = 2 * rows, 3 * rows, rows
    first = place_ref[0] == 0
    last = place_ref[0] == place_ref[1] - 1

    lane = lax.broadcasted_iota(jnp.int32, (1, rows), 1) // tok
    biases = []
    for j in range(2):
        start = jnp.zeros((1, rows), jnp.int32)
        for t in range(times):
            for h in range(2):
                start = jnp.where(lane == 2 * t + h, starts_ref[t, h, j], start)
        biases.append(
            [
                jnp.where((start <= t) & (t < start + 3), 0.0, NEG).astype(F32)
                for t in range(times)
            ]
        )

    def masked(scores, j):
        span = scores.shape[0] // times
        return [
            scores[t * span : (t + 1) * span] * (SCALE * LOG2E) + biases[j][t]
            for t in range(times)
        ]

    def load(index):
        cols = pl.ds(pl.multiple_of(index * HEAD_DIM, HEAD_DIM), HEAD_DIM)
        wide = pl.ds(pl.multiple_of((index + base) * HEAD_DIM, HEAD_DIM), HEAD_DIM)

        def flat(ref, *lead):
            lanes = wide if ref.shape[-1] == q_ref.shape[-1] else cols
            return ref[(*lead, lanes)].reshape(-1, HEAD_DIM)

        every = slice(None)
        q = jnp.concatenate([flat(q_ref, every, every, j, every) for j in range(2)], axis=0)
        g = jnp.concatenate([flat(g_ref, every, every, j, every) for j in range(2)], axis=0)
        own, side = [], []
        for s in range(2):
            own.append(
                jnp.concatenate(
                    [
                        flat(kv_ref, s, every, every, every, every),
                        flat(z_ref, s, every, every, every),
                    ],
                    axis=0,
                )
            )
            left = jnp.concatenate(
                [flat(xl_ref, s, every, every, every), flat(xlc_ref, s, every, every)], axis=0
            )
            right = jnp.concatenate(
                [flat(xr_ref, s, every, every, every), flat(xrc_ref, s, every, every)], axis=0
            )
            side.append((jnp.where(first, right, left), jnp.where(last, left, right)))
        return q, g, own, side

    def half(value, j):
        return value[j * rows : (j + 1) * rows]

    def products(loaded):
        q, g, own, side = loaded
        return (
            nt(own[0], q),
            nt(own[1], g),
            [nt(side[0][j], half(q, j)) for j in range(2)],
            [nt(side[1][j], half(g, j)) for j in range(2)],
        )

    def soften(made):
        s_own, p_own, s_x, p_x = made
        low_out, ds_out = [], []
        for j in range(2):
            lanes = slice(j * rows, (j + 1) * rows)
            parts = [s_own[:n_kv, lanes], s_own[n_kv:, lanes], s_x[j][:n_row], s_x[j][n_row:]]
            scores = jnp.concatenate(sum([masked(part, j) for part in parts], []), axis=0)
            grads = jnp.concatenate([p_own[:, lanes], p_x[j]], axis=0)
            top = jnp.max(scores, axis=0, keepdims=True)
            weights = jnp.exp2(scores - top)
            inverse = 1.0 / jnp.sum(weights, axis=0, keepdims=True)
            delta = jnp.sum(weights * grads, axis=0, keepdims=True) * inverse
            probs = weights * inverse
            low_out.append(probs.astype(BF))
            ds_out.append((probs * (grads - delta)).astype(BF))
        return low_out, ds_out

    def gradients(loaded, soft):
        q, g, own, side = loaded
        low, ds = soft
        d_own = (
            nn(jnp.concatenate([ds[0][:n_own], ds[1][:n_own]], axis=1), q) * SCALE,
            nn(jnp.concatenate([low[0][:n_own], low[1][:n_own]], axis=1), g),
        )
        dk_x = [nn(ds[j][n_own:], half(q, j)) * SCALE for j in range(2)]
        dv_x = [nn(low[j][n_own:], half(g, j)) for j in range(2)]
        dq = []
        for j in range(2):
            keys = jnp.concatenate([own[0], side[0][j]], axis=0)
            dq.append((tn(ds[j], keys) * SCALE).astype(BF))
        return d_own, (dk_x, dv_x), dq

    def store(cols, made):
        d_own, d_x, dq = made
        for j in range(2):
            dq_ref[:, :, j, :, cols] = dq[j].reshape(times, 2, tok, HEAD_DIM)
        for s in range(2):
            own_ref[s, :, :, :, :, cols] = (
                d_own[s][:n_kv].reshape(times, 2, 2, tok, HEAD_DIM).astype(own_ref.dtype)
            )
            dz_ref[s, :, :, :, cols] = d_own[s][n_kv:].reshape(times, 2, tok, HEAD_DIM)
            d0, d1 = d_x[s]
            left = (jnp.where(first, 0.0, d0) + jnp.where(last, d1, 0.0)).astype(BF)
            right = (jnp.where(last, 0.0, d1) + jnp.where(first, d0, 0.0)).astype(BF)
            for value, ref, corner in ((left, dxl_ref, dxlc_ref), (right, dxr_ref, dxrc_ref)):
                ref[s, :, :, :, cols] = value[:n_row].reshape(times, 2, tok, HEAD_DIM)
                corner[s, :, :, cols] = value[n_row:].reshape(times, tok, HEAD_DIM)

    def step(index, carry):
        each = [index * GROUP + i for i in range(GROUP)]
        loaded = [load(i) for i in each]
        made = [products(x) for x in loaded]
        soft = [soften(x) for x in made]
        done = [gradients(x, y) for x, y in zip(loaded, soft)]
        for i, d in zip(each, done):
            store(pl.ds(pl.multiple_of(i * HEAD_DIM, HEAD_DIM), HEAD_DIM), d)
        return carry

    lax.fori_loop(0, heads // GROUP, step, 0)


def corner_sum(dz_ref, c0_ref, c1_ref, out_ref):
    for j, ref in enumerate((c0_ref, c1_ref)):
        out_ref[:, :, j] = (dz_ref[:, :, j] + ref[...].astype(F32)).astype(BF)


def own_sum(own_ref, r0_ref, r1_ref, out_ref):
    for s in range(2):
        for j, ref in enumerate((r0_ref, r1_ref)):
            out_ref[s, :, :, j] = (own_ref[s, :, :, j] + ref[s].astype(F32)).astype(BF)


VMEM = pl.BlockSpec(memory_space=pltpu.VMEM)
SMEM = pl.BlockSpec(memory_space=pltpu.SMEM)


def call(body, specs, shapes, name, flops=0, moved=0, exps=0):
    single = not isinstance(shapes, (list, tuple))
    return pl.pallas_call(
        body,
        in_specs=specs,
        out_specs=VMEM if single else [VMEM] * len(shapes),
        out_shape=shapes,
        name=name,
        compiler_params=pltpu.CompilerParams(vmem_limit_bytes=58 * 2**20),
        cost_estimate=pl.CostEstimate(flops=flops, bytes_accessed=moved, transcendentals=exps),
    )


def local(queries, keys_values, grad_out, starts):
    queries, keys_values, grad_out = queries[0], keys_values[:, 0], grad_out[0]
    times, _, _, tok, channels = queries.shape
    row = lax.axis_index("ha")
    col = lax.axis_index("wa")
    col_place = jnp.stack([col, lax.axis_size("wa")]).astype(jnp.int32)
    sd = jax.ShapeDtypeStruct
    edge_row = lax.dynamic_index_in_dim(keys_values, 1 - row, axis=2, keepdims=False)

    halos = []
    base = 0
    own_done = z_done = corners_first = None
    for heads in CHUNKS:
        lanes = slice(base * HEAD_DIM, (base + heads) * HEAD_DIM)
        to_left = keys_values[:, :, :, 0, :, lanes]
        to_right = keys_values[:, :, :, 1, :, lanes]
        z_send = edge_row[..., lanes]
        if own_done is not None:
            gate = corners_first
            to_left, to_right, gate = lax.optimization_barrier((to_left, to_right, gate))
            z_send, z_done = lax.optimization_barrier((z_send, z_done))
        xr = shift(to_left, "wa", -1)
        xl = shift(to_right, "wa", 1)
        own_done = True
        z_row = z_done = shift(z_send, "ha", 1)
        if corners_first is None:
            xrc = shift(z_row[:, :, 0], "wa", -1)
            xlc = shift(z_row[:, :, 1], "wa", 1)
            corners_first = (xrc, xlc)
        halos.append((base, heads, z_row, xl, xr))
        base += heads

    made = []
    for index, (base, heads, z_row, xl, xr) in enumerate(halos):
        if index == 0:
            xrc, xlc = corners_first
        else:
            z_row, dq = lax.optimization_barrier((z_row, made[-1][0]))
            made[-1] = (dq, *made[-1][1:])
            xrc = shift(z_row[:, :, 0], "wa", -1)
            xlc = shift(z_row[:, :, 1], "wa", 1)
        width = heads * HEAD_DIM
        body = (times, 2, tok, width)
        outs = call(
            functools.partial(attend, base),
            [SMEM, SMEM] + [VMEM] * 8,
            [
                sd((times, 2, 2, tok, width), BF),
                sd((2, times, 2, 2, tok, width), F32),
                sd((2, *body), F32),
                sd((2, *body), BF),
                sd((2, times, tok, width), BF),
                sd((2, *body), BF),
                sd((2, times, tok, width), BF),
            ],
            "attend",
            flops=2 * 10**8 * heads,
            moved=2**20 * heads,
            exps=150000 * heads,
        )(col_place, starts, queries, grad_out, keys_values, z_row, xl, xlc, xr, xrc)
        made.append(outs)
    query_parts, pair_parts, across_parts = [], [], []
    z_back = total = None
    for index, (dq, own, dz, dxl, dxlc, dxr, dxrc) in enumerate(made):
        width = own.shape[-1]
        body = (times, 2, tok, width)
        query_part = shift(dq, "section", -1)
        if z_back is not None:
            dxlc, dxrc, z_back = lax.optimization_barrier((dxlc, dxrc, z_back))
            dxl, dxr, total = lax.optimization_barrier((dxl, dxr, total))
        r1c = shift(dxlc, "wa", -1)
        r0c = shift(dxrc, "wa", 1)
        r1 = shift(dxl, "wa", -1)
        r0 = shift(dxr, "wa", 1)
        z_back = call(corner_sum, [VMEM] * 3, sd((2, *body), BF), "corner_sum", moved=4 * 2**20)(
            dz, r0c, r1c
        )
        across = shift_across(z_back)
        held = (r0, r1, query_part, *across_parts)
        r0, r1, query_part, *across_parts = lax.optimization_barrier(held)
        total = call(
            own_sum, [VMEM] * 3, sd((2, times, 2, 2, tok, width), BF), "own_sum", moved=5 * 2**20
        )(own, r0, r1)
        query_parts.append(query_part)
        across_parts.append(across)
        pair_parts.append(shift(total, "section", -1))
    across = jnp.concatenate(across_parts, axis=-1)[:, :, None].astype(F32)
    pair = jnp.concatenate(pair_parts, axis=-1).astype(F32)
    at_edge = lax.broadcasted_iota(jnp.int32, (1, 1, 2, 1, 1, 1), 2) == 1 - row
    pair = (pair + jnp.where(at_edge, across, 0.0)).astype(BF)
    rows = [jnp.concatenate(query_parts, axis=-1)[None], pair]
    return jnp.concatenate(rows, axis=0)[:, None]


def solution(mesh):
    return jax.shard_map(
        local,
        mesh=mesh,
        in_specs=(
            P("section", None, "ha", "wa", None, None),
            P(None, "section", None, "ha", "wa", None, None),
            P("section", None, "ha", "wa", None, None),
            P(None, "ha", "wa"),
        ),
        out_specs=P(None, "section", None, "ha", "wa", None, None),
        check_vma=False,
    )
```

```python
import functools

import jax
import jax.numpy as jnp
from jax import lax
from jax.experimental import pallas as pl
from jax.experimental.pallas import tpu as pltpu
from jax.sharding import PartitionSpec as P

HEAD_DIM = 128
SCALE = HEAD_DIM**-0.5
LOG2E = 1.4426950408889634
CHUNKS = (12, 8)
NEG = -1e30
GROUP = 4
BF = jnp.bfloat16
F32 = jnp.float32


def shift(block, axis, step):
    count = lax.axis_size(axis)
    return lax.ppermute(block, axis, [(i, (i + step) % count) for i in range(count)])


def shift_across(block):
    sections = lax.axis_size("section")
    route = []
    for i in range(sections):
        for h in range(2):
            route.append((i * 2 + h, (i - 1) % sections * 2 + 1 - h))
    return lax.ppermute(block, ("section", "ha"), route)


def nt(a, b):
    return lax.dot_general(a, b, (((1,), (1,)), ((), ())), preferred_element_type=F32)


def nn(a, b):
    return lax.dot_general(a, b, (((1,), (0,)), ((), ())), preferred_element_type=F32)


def tn(a, b):
    return lax.dot_general(a, b, (((0,), (0,)), ((), ())), preferred_element_type=F32)


def attend(
    base, place_ref, starts_ref, q_ref, g_ref, kv_ref, z_ref, xl_ref, xlc_ref, xr_ref, xrc_ref,
    dq_ref, own_ref, dz_ref, dxl_ref, dxlc_ref, dxr_ref, dxrc_ref,
):
    times = q_ref.shape[0]
    tok = q_ref.shape[3]
    heads = dq_ref.shape[4] // HEAD_DIM
    rows = times * 2 * tok
    n_kv, n_own, n_row = 2 * rows, 3 * rows, rows
    first = place_ref[0] == 0
    last = place_ref[0] == place_ref[1] - 1

    lane = lax.broadcasted_iota(jnp.int32, (1, rows), 1) // tok
    biases = []
    for j in range(2):
        start = jnp.zeros((1, rows), jnp.int32)
        for t in range(times):
            for h in range(2):
                start = jnp.where(lane == 2 * t + h, starts_ref[t, h, j], start)
        biases.append(
            [
                jnp.where((start <= t) & (t < start + 3), 0.0, NEG).astype(F32)
                for t in range(times)
            ]
        )

    def masked(scores, j):
        span = scores.shape[0] // times
        return [
            scores[t * span : (t + 1) * span] * (SCALE * LOG2E) + biases[j][t]
            for t in range(times)
        ]

    def load(index):
        cols = pl.ds(pl.multiple_of(index * HEAD_DIM, HEAD_DIM), HEAD_DIM)
        wide = pl.ds(pl.multiple_of((index + base) * HEAD_DIM, HEAD_DIM), HEAD_DIM)

        def flat(ref, *lead):
            lanes = wide if ref.shape[-1] == q_ref.shape[-1] else cols
            return ref[(*lead, lanes)].reshape(-1, HEAD_DIM)

        every = slice(None)
        q = jnp.concatenate([flat(q_ref, every, every, j, every) for j in range(2)], axis=0)
        g = jnp.concatenate([flat(g_ref, every, every, j, every) for j in range(2)], axis=0)
        own, side = [], []
        for s in range(2):
            own.append(
                jnp.concatenate(
                    [
                        flat(kv_ref, s, every, every, every, every),
                        flat(z_ref, s, every, every, every),
                    ],
                    axis=0,
                )
            )
            left = jnp.concatenate(
                [flat(xl_ref, s, every, every, every), flat(xlc_ref, s, every, every)], axis=0
            )
            right = jnp.concatenate(
                [flat(xr_ref, s, every, every, every), flat(xrc_ref, s, every, every)], axis=0
            )
            side.append((jnp.where(first, right, left), jnp.where(last, left, right)))
        return q, g, own, side

    def half(value, j):
        return value[j * rows : (j + 1) * rows]

    def products(loaded):
        q, g, own, side = loaded
        return (
            nt(own[0], q),
            nt(own[1], g),
            [nt(side[0][j], half(q, j)) for j in range(2)],
            [nt(side[1][j], half(g, j)) for j in range(2)],
        )

    def soften(made):
        s_own, p_own, s_x, p_x = made
        low_out, ds_out = [], []
        for j in range(2):
            lanes = slice(j * rows, (j + 1) * rows)
            parts = [s_own[:n_kv, lanes], s_own[n_kv:, lanes], s_x[j][:n_row], s_x[j][n_row:]]
            scores = jnp.concatenate(sum([masked(part, j) for part in parts], []), axis=0)
            grads = jnp.concatenate([p_own[:, lanes], p_x[j]], axis=0)
            top = jnp.max(scores, axis=0, keepdims=True)
            weights = jnp.exp2(scores - top)
            inverse = 1.0 / jnp.sum(weights, axis=0, keepdims=True)
            delta = jnp.sum(weights * grads, axis=0, keepdims=True) * inverse
            probs = weights * inverse
            low_out.append(probs.astype(BF))
            ds_out.append((probs * (grads - delta)).astype(BF))
        return low_out, ds_out

    def gradients(loaded, soft):
        q, g, own, side = loaded
        low, ds = soft
        d_own = (
            nn(jnp.concatenate([ds[0][:n_own], ds[1][:n_own]], axis=1), q) * SCALE,
            nn(jnp.concatenate([low[0][:n_own], low[1][:n_own]], axis=1), g),
        )
        dk_x = [nn(ds[j][n_own:], half(q, j)) * SCALE for j in range(2)]
        dv_x = [nn(low[j][n_own:], half(g, j)) for j in range(2)]
        dq = []
        for j in range(2):
            keys = jnp.concatenate([own[0], side[0][j]], axis=0)
            dq.append((tn(ds[j], keys) * SCALE).astype(BF))
        return d_own, (dk_x, dv_x), dq

    def store(cols, made):
        d_own, d_x, dq = made
        for j in range(2):
            dq_ref[:, :, j, :, cols] = dq[j].reshape(times, 2, tok, HEAD_DIM)
        for s in range(2):
            own_ref[s, :, :, :, :, cols] = (
                d_own[s][:n_kv].reshape(times, 2, 2, tok, HEAD_DIM).astype(own_ref.dtype)
            )
            dz_ref[s, :, :, :, cols] = d_own[s][n_kv:].reshape(times, 2, tok, HEAD_DIM)
            d0, d1 = d_x[s]
            left = (jnp.where(first, 0.0, d0) + jnp.where(last, d1, 0.0)).astype(BF)
            right = (jnp.where(last, 0.0, d1) + jnp.where(first, d0, 0.0)).astype(BF)
            for value, ref, corner in ((left, dxl_ref, dxlc_ref), (right, dxr_ref, dxrc_ref)):
                ref[s, :, :, :, cols] = value[:n_row].reshape(times, 2, tok, HEAD_DIM)
                corner[s, :, :, cols] = value[n_row:].reshape(times, tok, HEAD_DIM)

    def step(index, carry):
        each = [index * GROUP + i for i in range(GROUP)]
        loaded = [load(i) for i in each]
        made = [products(loaded[0])]
        for n, i in enumerate(each):
            if n + 1 < GROUP:
                made.append(products(loaded[n + 1]))
            done = gradients(loaded[n], soften(made[n]))
            store(pl.ds(pl.multiple_of(i * HEAD_DIM, HEAD_DIM), HEAD_DIM), done)
        return carry

    lax.fori_loop(0, heads // GROUP, step, 0)


def corner_sum(dz_ref, c0_ref, c1_ref, out_ref):
    for j, ref in enumerate((c0_ref, c1_ref)):
        out_ref[:, :, j] = (dz_ref[:, :, j] + ref[...].astype(F32)).astype(BF)


def own_sum(own_ref, r0_ref, r1_ref, out_ref):
    for s in range(2):
        for j, ref in enumerate((r0_ref, r1_ref)):
            out_ref[s, :, :, j] = (own_ref[s, :, :, j].astype(F32) + ref[s].astype(F32)).astype(BF)


VMEM = pl.BlockSpec(memory_space=pltpu.VMEM)
SMEM = pl.BlockSpec(memory_space=pltpu.SMEM)


def call(body, specs, shapes, name, flops=0, moved=0, exps=0):
    single = not isinstance(shapes, (list, tuple))
    return pl.pallas_call(
        body,
        in_specs=specs,
        out_specs=VMEM if single else [VMEM] * len(shapes),
        out_shape=shapes,
        name=name,
        compiler_params=pltpu.CompilerParams(vmem_limit_bytes=58 * 2**20),
        cost_estimate=pl.CostEstimate(flops=flops, bytes_accessed=moved, transcendentals=exps),
    )


def local(queries, keys_values, grad_out, starts):
    queries, keys_values, grad_out = queries[0], keys_values[:, 0], grad_out[0]
    times, _, _, tok, channels = queries.shape
    row = lax.axis_index("ha")
    col = lax.axis_index("wa")
    col_place = jnp.stack([col, lax.axis_size("wa")]).astype(jnp.int32)
    sd = jax.ShapeDtypeStruct
    edge_row = lax.dynamic_index_in_dim(keys_values, 1 - row, axis=2, keepdims=False)

    halos = []
    base = 0
    own_done = z_done = corners_first = None
    for heads in CHUNKS:
        lanes = slice(base * HEAD_DIM, (base + heads) * HEAD_DIM)
        to_left = keys_values[:, :, :, 0, :, lanes]
        to_right = keys_values[:, :, :, 1, :, lanes]
        z_send = edge_row[..., lanes]
        if own_done is not None:
            gate = corners_first
            to_left, to_right, gate = lax.optimization_barrier((to_left, to_right, gate))
            z_send, z_done = lax.optimization_barrier((z_send, z_done))
        xr = shift(to_left, "wa", -1)
        xl = shift(to_right, "wa", 1)
        own_done = True
        z_row = z_done = shift(z_send, "ha", 1)
        if corners_first is None:
            xrc = shift(z_row[:, :, 0], "wa", -1)
            xlc = shift(z_row[:, :, 1], "wa", 1)
            corners_first = (xrc, xlc)
        halos.append((base, heads, z_row, xl, xr))
        base += heads

    made = []
    for index, (base, heads, z_row, xl, xr) in enumerate(halos):
        if index == 0:
            xrc, xlc = corners_first
        else:
            z_row, dq = lax.optimization_barrier((z_row, made[-1][0]))
            made[-1] = (dq, *made[-1][1:])
            xrc = shift(z_row[:, :, 0], "wa", -1)
            xlc = shift(z_row[:, :, 1], "wa", 1)
        width = heads * HEAD_DIM
        body = (times, 2, tok, width)
        outs = call(
            functools.partial(attend, base),
            [SMEM, SMEM] + [VMEM] * 8,
            [
                sd((times, 2, 2, tok, width), BF),
                sd((2, times, 2, 2, tok, width), BF),
                sd((2, *body), F32),
                sd((2, *body), BF),
                sd((2, times, tok, width), BF),
                sd((2, *body), BF),
                sd((2, times, tok, width), BF),
            ],
            "attend",
            flops=2 * 10**8 * heads,
            moved=2**20 * heads,
            exps=150000 * heads,
        )(col_place, starts, queries, grad_out, keys_values, z_row, xl, xlc, xr, xrc)
        made.append(outs)
    query_parts, pair_parts, across_parts = [], [], []
    z_back = total = None
    for index, (dq, own, dz, dxl, dxlc, dxr, dxrc) in enumerate(made):
        width = own.shape[-1]
        body = (times, 2, tok, width)
        query_part = shift(dq, "section", -1)
        if z_back is not None:
            dxlc, dxrc, z_back = lax.optimization_barrier((dxlc, dxrc, z_back))
            dxl, dxr, total = lax.optimization_barrier((dxl, dxr, total))
        r1c = shift(dxlc, "wa", -1)
        r0c = shift(dxrc, "wa", 1)
        r1 = shift(dxl, "wa", -1)
        r0 = shift(dxr, "wa", 1)
        z_back = call(corner_sum, [VMEM] * 3, sd((2, *body), BF), "corner_sum", moved=4 * 2**20)(
            dz, r0c, r1c
        )
        across = shift_across(z_back)
        held = (r0, r1, query_part, *across_parts)
        r0, r1, query_part, *across_parts = lax.optimization_barrier(held)
        total = call(
            own_sum, [VMEM] * 3, sd((2, times, 2, 2, tok, width), BF), "own_sum", moved=5 * 2**20
        )(own, r0, r1)
        query_parts.append(query_part)
        across_parts.append(across)
        pair_parts.append(shift(total, "section", -1))
    across = jnp.concatenate(across_parts, axis=-1)[:, :, None].astype(F32)
    pair = jnp.concatenate(pair_parts, axis=-1).astype(F32)
    at_edge = lax.broadcasted_iota(jnp.int32, (1, 1, 2, 1, 1, 1), 2) == 1 - row
    pair = (pair + jnp.where(at_edge, across, 0.0)).astype(BF)
    rows = [jnp.concatenate(query_parts, axis=-1)[None], pair]
    return jnp.concatenate(rows, axis=0)[:, None]


def solution(mesh):
    return jax.shard_map(
        local,
        mesh=mesh,
        in_specs=(
            P("section", None, "ha", "wa", None, None),
            P(None, "section", None, "ha", "wa", None, None),
            P("section", None, "ha", "wa", None, None),
            P(None, "ha", "wa"),
        ),
        out_specs=P(None, "section", None, "ha", "wa", None, None),
        check_vma=False,
    )
```

```python
import functools

import jax
import jax.numpy as jnp
from jax import lax
from jax.experimental import pallas as pl
from jax.experimental.pallas import tpu as pltpu
from jax.sharding import PartitionSpec as P

HEAD_DIM = 128
SCALE = HEAD_DIM**-0.5
LOG2E = 1.4426950408889634
CHUNKS = (12, 8)
NEG = -1e30
GROUP = 4
BF = jnp.bfloat16
F32 = jnp.float32


def shift(block, axis, step):
    count = lax.axis_size(axis)
    return lax.ppermute(block, axis, [(i, (i + step) % count) for i in range(count)])


def shift_across(block):
    sections = lax.axis_size("section")
    route = []
    for i in range(sections):
        for h in range(2):
            route.append((i * 2 + h, (i - 1) % sections * 2 + 1 - h))
    return lax.ppermute(block, ("section", "ha"), route)


def nt(a, b):
    return lax.dot_general(a, b, (((1,), (1,)), ((), ())), preferred_element_type=F32)


def nn(a, b):
    return lax.dot_general(a, b, (((1,), (0,)), ((), ())), preferred_element_type=F32)


def tn(a, b):
    return lax.dot_general(a, b, (((0,), (0,)), ((), ())), preferred_element_type=F32)


def attend(
    base, place_ref, starts_ref, q_ref, g_ref, kv_ref, z_ref, xl_ref, xlc_ref, xr_ref, xrc_ref,
    dq_ref, own_ref, dz_ref, dxl_ref, dxlc_ref, dxr_ref, dxrc_ref,
):
    times = q_ref.shape[0]
    tok = q_ref.shape[3]
    heads = dq_ref.shape[4] // HEAD_DIM
    rows = times * 2 * tok
    n_kv, n_own, n_row = 2 * rows, 3 * rows, rows
    first = place_ref[0] == 0
    last = place_ref[0] == place_ref[1] - 1

    lane = lax.broadcasted_iota(jnp.int32, (1, rows), 1) // tok
    biases = []
    for j in range(2):
        start = jnp.zeros((1, rows), jnp.int32)
        for t in range(times):
            for h in range(2):
                start = jnp.where(lane == 2 * t + h, starts_ref[t, h, j], start)
        biases.append(
            [
                jnp.where((start <= t) & (t < start + 3), 0.0, NEG).astype(F32)
                for t in range(times)
            ]
        )

    def masked(scores, j):
        span = scores.shape[0] // times
        return [
            scores[t * span : (t + 1) * span] * (SCALE * LOG2E) + biases[j][t]
            for t in range(times)
        ]

    def load(index):
        cols = pl.ds(pl.multiple_of(index * HEAD_DIM, HEAD_DIM), HEAD_DIM)
        wide = pl.ds(pl.multiple_of((index + base) * HEAD_DIM, HEAD_DIM), HEAD_DIM)

        def flat(ref, *lead):
            lanes = wide if ref.shape[-1] == q_ref.shape[-1] else cols
            return ref[(*lead, lanes)].reshape(-1, HEAD_DIM)

        every = slice(None)
        q = jnp.concatenate([flat(q_ref, every, every, j, every) for j in range(2)], axis=0)
        g = jnp.concatenate([flat(g_ref, every, every, j, every) for j in range(2)], axis=0)
        own, side = [], []
        for s in range(2):
            own.append(
                jnp.concatenate(
                    [
                        flat(kv_ref, s, every, every, every, every),
                        flat(z_ref, s, every, every, every),
                    ],
                    axis=0,
                )
            )
            left = jnp.concatenate(
                [flat(xl_ref, s, every, every, every), flat(xlc_ref, s, every, every)], axis=0
            )
            right = jnp.concatenate(
                [flat(xr_ref, s, every, every, every), flat(xrc_ref, s, every, every)], axis=0
            )
            side.append((jnp.where(first, right, left), jnp.where(last, left, right)))
        return q, g, own, side

    def half(value, j):
        return value[j * rows : (j + 1) * rows]

    def products(loaded):
        q, g, own, side = loaded
        return (
            nt(own[0], q),
            nt(own[1], g),
            [nt(side[0][j], half(q, j)) for j in range(2)],
            [nt(side[1][j], half(g, j)) for j in range(2)],
        )

    def soften(made):
        s_own, p_own, s_x, p_x = made
        low_out, ds_out = [], []
        for j in range(2):
            lanes = slice(j * rows, (j + 1) * rows)
            parts = [s_own[:n_kv, lanes], s_own[n_kv:, lanes], s_x[j][:n_row], s_x[j][n_row:]]
            scores = jnp.concatenate(sum([masked(part, j) for part in parts], []), axis=0)
            grads = jnp.concatenate([p_own[:, lanes], p_x[j]], axis=0)
            top = jnp.max(scores, axis=0, keepdims=True)
            weights = jnp.exp2(scores - top)
            inverse = 1.0 / jnp.sum(weights, axis=0, keepdims=True)
            delta = jnp.sum(weights * grads, axis=0, keepdims=True) * inverse
            probs = weights * inverse
            low_out.append(probs.astype(BF))
            ds_out.append((probs * (grads - delta)).astype(BF))
        return low_out, ds_out

    def gradients(loaded, soft):
        q, g, own, side = loaded
        low, ds = soft
        d_own = (
            nn(jnp.concatenate([ds[0][:n_own], ds[1][:n_own]], axis=1), q) * SCALE,
            nn(jnp.concatenate([low[0][:n_own], low[1][:n_own]], axis=1), g),
        )
        dk_x = [nn(ds[j][n_own:], half(q, j)) * SCALE for j in range(2)]
        dv_x = [nn(low[j][n_own:], half(g, j)) for j in range(2)]
        dq = []
        for j in range(2):
            keys = jnp.concatenate([own[0], side[0][j]], axis=0)
            dq.append((tn(ds[j], keys) * SCALE).astype(BF))
        return d_own, (dk_x, dv_x), dq

    def store(cols, made):
        d_own, d_x, dq = made
        for j in range(2):
            dq_ref[:, :, j, :, cols] = dq[j].reshape(times, 2, tok, HEAD_DIM)
        for s in range(2):
            own_ref[s, :, :, :, :, cols] = (
                d_own[s][:n_kv].reshape(times, 2, 2, tok, HEAD_DIM).astype(own_ref.dtype)
            )
            dz_ref[s, :, :, :, cols] = d_own[s][n_kv:].reshape(times, 2, tok, HEAD_DIM).astype(BF)
            d0, d1 = d_x[s]
            left = (jnp.where(first, 0.0, d0) + jnp.where(last, d1, 0.0)).astype(BF)
            right = (jnp.where(last, 0.0, d1) + jnp.where(first, d0, 0.0)).astype(BF)
            for value, ref, corner in ((left, dxl_ref, dxlc_ref), (right, dxr_ref, dxrc_ref)):
                ref[s, :, :, :, cols] = value[:n_row].reshape(times, 2, tok, HEAD_DIM)
                corner[s, :, :, cols] = value[n_row:].reshape(times, tok, HEAD_DIM)

    def step(index, carry):
        each = [index * GROUP + i for i in range(GROUP)]
        loaded = [load(i) for i in each]
        made = [products(loaded[0])]
        for n, i in enumerate(each):
            if n + 1 < GROUP:
                made.append(products(loaded[n + 1]))
            done = gradients(loaded[n], soften(made[n]))
            store(pl.ds(pl.multiple_of(i * HEAD_DIM, HEAD_DIM), HEAD_DIM), done)
        return carry

    lax.fori_loop(0, heads // GROUP, step, 0)


def corner_sum(dz_ref, c0_ref, c1_ref, out_ref):
    for j, ref in enumerate((c0_ref, c1_ref)):
        out_ref[:, :, j] = (dz_ref[:, :, j].astype(F32) + ref[...].astype(F32)).astype(BF)


def own_sum(own_ref, r0_ref, r1_ref, out_ref):
    for s in range(2):
        for j, ref in enumerate((r0_ref, r1_ref)):
            out_ref[s, :, :, j] = (own_ref[s, :, :, j].astype(F32) + ref[s].astype(F32)).astype(BF)


VMEM = pl.BlockSpec(memory_space=pltpu.VMEM)
SMEM = pl.BlockSpec(memory_space=pltpu.SMEM)


def call(body, specs, shapes, name, flops=0, moved=0, exps=0):
    single = not isinstance(shapes, (list, tuple))
    return pl.pallas_call(
        body,
        in_specs=specs,
        out_specs=VMEM if single else [VMEM] * len(shapes),
        out_shape=shapes,
        name=name,
        compiler_params=pltpu.CompilerParams(vmem_limit_bytes=58 * 2**20),
        cost_estimate=pl.CostEstimate(flops=flops, bytes_accessed=moved, transcendentals=exps),
    )


def local(queries, keys_values, grad_out, starts):
    queries, keys_values, grad_out = queries[0], keys_values[:, 0], grad_out[0]
    times, _, _, tok, channels = queries.shape
    row = lax.axis_index("ha")
    col = lax.axis_index("wa")
    col_place = jnp.stack([col, lax.axis_size("wa")]).astype(jnp.int32)
    sd = jax.ShapeDtypeStruct
    edge_row = lax.dynamic_index_in_dim(keys_values, 1 - row, axis=2, keepdims=False)

    halos = []
    base = 0
    own_done = z_done = corners_first = None
    for heads in CHUNKS:
        lanes = slice(base * HEAD_DIM, (base + heads) * HEAD_DIM)
        to_left = keys_values[:, :, :, 0, :, lanes]
        to_right = keys_values[:, :, :, 1, :, lanes]
        z_send = edge_row[..., lanes]
        if own_done is not None:
            gate = corners_first
            to_left, to_right, gate = lax.optimization_barrier((to_left, to_right, gate))
            z_send, z_done = lax.optimization_barrier((z_send, z_done))
        xr = shift(to_left, "wa", -1)
        xl = shift(to_right, "wa", 1)
        own_done = True
        z_row = z_done = shift(z_send, "ha", 1)
        if corners_first is None:
            xrc = shift(z_row[:, :, 0], "wa", -1)
            xlc = shift(z_row[:, :, 1], "wa", 1)
            corners_first = (xrc, xlc)
        halos.append((base, heads, z_row, xl, xr))
        base += heads

    made = []
    for index, (base, heads, z_row, xl, xr) in enumerate(halos):
        if index == 0:
            xrc, xlc = corners_first
        else:
            z_row, dq = lax.optimization_barrier((z_row, made[-1][0]))
            made[-1] = (dq, *made[-1][1:])
            xrc = shift(z_row[:, :, 0], "wa", -1)
            xlc = shift(z_row[:, :, 1], "wa", 1)
        width = heads * HEAD_DIM
        body = (times, 2, tok, width)
        outs = call(
            functools.partial(attend, base),
            [SMEM, SMEM] + [VMEM] * 8,
            [
                sd((times, 2, 2, tok, width), BF),
                sd((2, times, 2, 2, tok, width), BF),
                sd((2, *body), BF),
                sd((2, *body), BF),
                sd((2, times, tok, width), BF),
                sd((2, *body), BF),
                sd((2, times, tok, width), BF),
            ],
            "attend",
            flops=2 * 10**8 * heads,
            moved=2**20 * heads,
            exps=150000 * heads,
        )(col_place, starts, queries, grad_out, keys_values, z_row, xl, xlc, xr, xrc)
        made.append(outs)
    query_parts, pair_parts, across_parts = [], [], []
    z_back = total = None
    for index, (dq, own, dz, dxl, dxlc, dxr, dxrc) in enumerate(made):
        width = own.shape[-1]
        body = (times, 2, tok, width)
        query_part = shift(dq, "section", -1)
        if z_back is not None:
            dxlc, dxrc, z_back = lax.optimization_barrier((dxlc, dxrc, z_back))
            dxl, dxr, total = lax.optimization_barrier((dxl, dxr, total))
        r1c = shift(dxlc, "wa", -1)
        r0c = shift(dxrc, "wa", 1)
        r1 = shift(dxl, "wa", -1)
        r0 = shift(dxr, "wa", 1)
        z_back = call(corner_sum, [VMEM] * 3, sd((2, *body), BF), "corner_sum", moved=4 * 2**20)(
            dz, r0c, r1c
        )
        across = shift_across(z_back)
        held = (r0, r1, query_part, *across_parts)
        r0, r1, query_part, *across_parts = lax.optimization_barrier(held)
        total = call(
            own_sum, [VMEM] * 3, sd((2, times, 2, 2, tok, width), BF), "own_sum", moved=5 * 2**20
        )(own, r0, r1)
        query_parts.append(query_part)
        across_parts.append(across)
        pair_parts.append(shift(total, "section", -1))
    across = jnp.concatenate(across_parts, axis=-1)[:, :, None].astype(F32)
    pair = jnp.concatenate(pair_parts, axis=-1).astype(F32)
    at_edge = lax.broadcasted_iota(jnp.int32, (1, 1, 2, 1, 1, 1), 2) == 1 - row
    pair = (pair + jnp.where(at_edge, across, 0.0)).astype(BF)
    rows = [jnp.concatenate(query_parts, axis=-1)[None], pair]
    return jnp.concatenate(rows, axis=0)[:, None]


def solution(mesh):
    return jax.shard_map(
        local,
        mesh=mesh,
        in_specs=(
            P("section", None, "ha", "wa", None, None),
            P(None, "section", None, "ha", "wa", None, None),
            P("section", None, "ha", "wa", None, None),
            P(None, "ha", "wa"),
        ),
        out_specs=P(None, "section", None, "ha", "wa", None, None),
        check_vma=False,
    )
```

```python
import functools

import jax
import jax.numpy as jnp
from jax import lax
from jax.experimental import pallas as pl
from jax.experimental.pallas import tpu as pltpu
from jax.sharding import PartitionSpec as P

HEAD_DIM = 128
SCALE = HEAD_DIM**-0.5
LOG2E = 1.4426950408889634
CHUNKS = (12, 8)
NEG = -1e30
GROUP = 4
BF = jnp.bfloat16
F32 = jnp.float32


def shift(block, axis, step):
    count = lax.axis_size(axis)
    return lax.ppermute(block, axis, [(i, (i + step) % count) for i in range(count)])


def shift_across(block):
    sections = lax.axis_size("section")
    route = []
    for i in range(sections):
        for h in range(2):
            route.append((i * 2 + h, (i - 1) % sections * 2 + 1 - h))
    return lax.ppermute(block, ("section", "ha"), route)


def nt(a, b):
    return lax.dot_general(a, b, (((1,), (1,)), ((), ())), preferred_element_type=F32)


def nn(a, b):
    return lax.dot_general(a, b, (((1,), (0,)), ((), ())), preferred_element_type=F32)


def tn(a, b):
    return lax.dot_general(a, b, (((0,), (0,)), ((), ())), preferred_element_type=F32)


def attend(
    base, place_ref, starts_ref, q_ref, g_ref, kv_ref, z_ref, xl_ref, xlc_ref, xr_ref, xrc_ref,
    dq_ref, own_ref, dz_ref, dxl_ref, dxlc_ref, dxr_ref, dxrc_ref,
):
    times = q_ref.shape[0]
    tok = q_ref.shape[3]
    heads = dq_ref.shape[4] // HEAD_DIM
    rows = times * 2 * tok
    n_kv, n_own, n_row = 2 * rows, 3 * rows, rows
    first = place_ref[0] == 0
    last = place_ref[0] == place_ref[1] - 1

    lane = lax.broadcasted_iota(jnp.int32, (1, rows), 1) // tok
    biases = []
    for j in range(2):
        start = jnp.zeros((1, rows), jnp.int32)
        for t in range(times):
            for h in range(2):
                start = jnp.where(lane == 2 * t + h, starts_ref[t, h, j], start)
        biases.append(
            [
                jnp.where((start <= t) & (t < start + 3), 0.0, NEG).astype(F32)
                for t in range(times)
            ]
        )

    def masked(scores, j):
        span = scores.shape[0] // times
        return [
            scores[t * span : (t + 1) * span] * (SCALE * LOG2E) + biases[j][t]
            for t in range(times)
        ]

    def load(index):
        cols = pl.ds(pl.multiple_of(index * HEAD_DIM, HEAD_DIM), HEAD_DIM)
        wide = pl.ds(pl.multiple_of((index + base) * HEAD_DIM, HEAD_DIM), HEAD_DIM)

        def flat(ref, *lead):
            lanes = wide if ref.shape[-1] == q_ref.shape[-1] else cols
            return ref[(*lead, lanes)].reshape(-1, HEAD_DIM)

        every = slice(None)
        q = jnp.concatenate([flat(q_ref, every, every, j, every) for j in range(2)], axis=0)
        g = jnp.concatenate([flat(g_ref, every, every, j, every) for j in range(2)], axis=0)
        own, side = [], []
        for s in range(2):
            own.append(
                jnp.concatenate(
                    [
                        flat(kv_ref, s, every, every, every, every),
                        flat(z_ref, s, every, every, every),
                    ],
                    axis=0,
                )
            )
            left = jnp.concatenate(
                [flat(xl_ref, s, every, every, every), flat(xlc_ref, s, every, every)], axis=0
            )
            right = jnp.concatenate(
                [flat(xr_ref, s, every, every, every), flat(xrc_ref, s, every, every)], axis=0
            )
            side.append((jnp.where(first, right, left), jnp.where(last, left, right)))
        return q, g, own, side

    def half(value, j):
        return value[j * rows : (j + 1) * rows]

    def products(loaded):
        q, g, own, side = loaded
        return (
            nt(own[0], q),
            nt(own[1], g),
            [nt(side[0][j], half(q, j)) for j in range(2)],
            [nt(side[1][j], half(g, j)) for j in range(2)],
        )

    def soften(made):
        s_own, p_own, s_x, p_x = made
        low_out, ds_out = [], []
        for j in range(2):
            lanes = slice(j * rows, (j + 1) * rows)
            parts = [s_own[:n_kv, lanes], s_own[n_kv:, lanes], s_x[j][:n_row], s_x[j][n_row:]]
            scores = jnp.concatenate(sum([masked(part, j) for part in parts], []), axis=0)
            grads = jnp.concatenate([p_own[:, lanes], p_x[j]], axis=0)
            top = jnp.max(scores, axis=0, keepdims=True)
            weights = jnp.exp2(scores - top)
            inverse = 1.0 / jnp.sum(weights, axis=0, keepdims=True)
            delta = jnp.sum(weights * grads, axis=0, keepdims=True) * inverse
            probs = weights * inverse
            low_out.append(probs.astype(BF))
            ds_out.append((probs * (grads - delta)).astype(BF))
        return low_out, ds_out

    def gradients(loaded, soft):
        q, g, own, side = loaded
        low, ds = soft
        d_own = (
            nn(jnp.concatenate([ds[0][:n_own], ds[1][:n_own]], axis=1), q) * SCALE,
            nn(jnp.concatenate([low[0][:n_own], low[1][:n_own]], axis=1), g),
        )
        dk_x = [nn(ds[j][n_own:], half(q, j)) * SCALE for j in range(2)]
        dv_x = [nn(low[j][n_own:], half(g, j)) for j in range(2)]
        dq = []
        for j in range(2):
            keys = jnp.concatenate([own[0], side[0][j]], axis=0)
            dq.append((tn(ds[j], keys) * SCALE).astype(BF))
        return d_own, (dk_x, dv_x), dq

    def store(cols, made):
        d_own, d_x, dq = made
        for j in range(2):
            dq_ref[:, :, j, :, cols] = dq[j].reshape(times, 2, tok, HEAD_DIM)
        for s in range(2):
            own_ref[s, :, :, :, :, cols] = (
                d_own[s][:n_kv].reshape(times, 2, 2, tok, HEAD_DIM).astype(own_ref.dtype)
            )
            dz_ref[s, :, :, :, cols] = d_own[s][n_kv:].reshape(times, 2, tok, HEAD_DIM)
            d0, d1 = d_x[s]
            both, none = (d0 + d1).astype(BF), jnp.zeros_like(d0, BF)
            left = jnp.where(first, none, jnp.where(last, both, d0.astype(BF)))
            right = jnp.where(last, none, jnp.where(first, both, d1.astype(BF)))
            for value, ref, corner in ((left, dxl_ref, dxlc_ref), (right, dxr_ref, dxrc_ref)):
                ref[s, :, :, :, cols] = value[:n_row].reshape(times, 2, tok, HEAD_DIM)
                corner[s, :, :, cols] = value[n_row:].reshape(times, tok, HEAD_DIM)

    def step(index, carry):
        each = [index * GROUP + i for i in range(GROUP)]
        loaded = [load(i) for i in each]
        made = [products(loaded[0])]
        for n, i in enumerate(each):
            if n + 1 < GROUP:
                made.append(products(loaded[n + 1]))
            done = gradients(loaded[n], soften(made[n]))
            store(pl.ds(pl.multiple_of(i * HEAD_DIM, HEAD_DIM), HEAD_DIM), done)
        return carry

    lax.fori_loop(0, heads // GROUP, step, 0)


def corner_sum(dz_ref, c0_ref, c1_ref, out_ref):
    for j, ref in enumerate((c0_ref, c1_ref)):
        out_ref[:, :, j] = (dz_ref[:, :, j] + ref[...].astype(F32)).astype(BF)


def own_sum(own_ref, r0_ref, r1_ref, out_ref):
    for s in range(2):
        for j, ref in enumerate((r0_ref, r1_ref)):
            out_ref[s, :, :, j] = (own_ref[s, :, :, j].astype(F32) + ref[s].astype(F32)).astype(BF)


VMEM = pl.BlockSpec(memory_space=pltpu.VMEM)
SMEM = pl.BlockSpec(memory_space=pltpu.SMEM)


def call(body, specs, shapes, name, flops=0, moved=0, exps=0):
    single = not isinstance(shapes, (list, tuple))
    return pl.pallas_call(
        body,
        in_specs=specs,
        out_specs=VMEM if single else [VMEM] * len(shapes),
        out_shape=shapes,
        name=name,
        compiler_params=pltpu.CompilerParams(vmem_limit_bytes=58 * 2**20),
        cost_estimate=pl.CostEstimate(flops=flops, bytes_accessed=moved, transcendentals=exps),
    )


def local(queries, keys_values, grad_out, starts):
    queries, keys_values, grad_out = queries[0], keys_values[:, 0], grad_out[0]
    times, _, _, tok, channels = queries.shape
    row = lax.axis_index("ha")
    col = lax.axis_index("wa")
    col_place = jnp.stack([col, lax.axis_size("wa")]).astype(jnp.int32)
    sd = jax.ShapeDtypeStruct
    edge_row = lax.dynamic_index_in_dim(keys_values, 1 - row, axis=2, keepdims=False)

    halos = []
    base = 0
    own_done = z_done = corners_first = None
    for heads in CHUNKS:
        lanes = slice(base * HEAD_DIM, (base + heads) * HEAD_DIM)
        to_left = keys_values[:, :, :, 0, :, lanes]
        to_right = keys_values[:, :, :, 1, :, lanes]
        z_send = edge_row[..., lanes]
        if own_done is not None:
            gate = corners_first
            to_left, to_right, gate = lax.optimization_barrier((to_left, to_right, gate))
            z_send, z_done = lax.optimization_barrier((z_send, z_done))
        xr = shift(to_left, "wa", -1)
        xl = shift(to_right, "wa", 1)
        own_done = True
        z_row = z_done = shift(z_send, "ha", 1)
        if corners_first is None:
            xrc = shift(z_row[:, :, 0], "wa", -1)
            xlc = shift(z_row[:, :, 1], "wa", 1)
            corners_first = (xrc, xlc)
        halos.append((base, heads, z_row, xl, xr))
        base += heads

    made = []
    for index, (base, heads, z_row, xl, xr) in enumerate(halos):
        if index == 0:
            xrc, xlc = corners_first
        else:
            z_row, dq = lax.optimization_barrier((z_row, made[-1][0]))
            made[-1] = (dq, *made[-1][1:])
            xrc = shift(z_row[:, :, 0], "wa", -1)
            xlc = shift(z_row[:, :, 1], "wa", 1)
        width = heads * HEAD_DIM
        body = (times, 2, tok, width)
        outs = call(
            functools.partial(attend, base),
            [SMEM, SMEM] + [VMEM] * 8,
            [
                sd((times, 2, 2, tok, width), BF),
                sd((2, times, 2, 2, tok, width), BF),
                sd((2, *body), F32),
                sd((2, *body), BF),
                sd((2, times, tok, width), BF),
                sd((2, *body), BF),
                sd((2, times, tok, width), BF),
            ],
            "attend",
            flops=2 * 10**8 * heads,
            moved=2**20 * heads,
            exps=150000 * heads,
        )(col_place, starts, queries, grad_out, keys_values, z_row, xl, xlc, xr, xrc)
        made.append(outs)
    query_parts, pair_parts, across_parts = [], [], []
    z_back = total = None
    for index, (dq, own, dz, dxl, dxlc, dxr, dxrc) in enumerate(made):
        width = own.shape[-1]
        body = (times, 2, tok, width)
        query_part = shift(dq, "section", -1)
        if z_back is not None:
            dxlc, dxrc, z_back = lax.optimization_barrier((dxlc, dxrc, z_back))
            dxl, dxr, total = lax.optimization_barrier((dxl, dxr, total))
        r1c = shift(dxlc, "wa", -1)
        r0c = shift(dxrc, "wa", 1)
        r1 = shift(dxl, "wa", -1)
        r0 = shift(dxr, "wa", 1)
        z_back = call(corner_sum, [VMEM] * 3, sd((2, *body), BF), "corner_sum", moved=4 * 2**20)(
            dz, r0c, r1c
        )
        across = shift_across(z_back)
        held = (r0, r1, query_part, *across_parts)
        r0, r1, query_part, *across_parts = lax.optimization_barrier(held)
        total = call(
            own_sum, [VMEM] * 3, sd((2, times, 2, 2, tok, width), BF), "own_sum", moved=5 * 2**20
        )(own, r0, r1)
        query_parts.append(query_part)
        across_parts.append(across)
        pair_parts.append(shift(total, "section", -1))
    across = jnp.concatenate(across_parts, axis=-1)[:, :, None].astype(F32)
    pair = jnp.concatenate(pair_parts, axis=-1).astype(F32)
    at_edge = lax.broadcasted_iota(jnp.int32, (1, 1, 2, 1, 1, 1), 2) == 1 - row
    pair = (pair + jnp.where(at_edge, across, 0.0)).astype(BF)
    rows = [jnp.concatenate(query_parts, axis=-1)[None], pair]
    return jnp.concatenate(rows, axis=0)[:, None]


def solution(mesh):
    return jax.shard_map(
        local,
        mesh=mesh,
        in_specs=(
            P("section", None, "ha", "wa", None, None),
            P(None, "section", None, "ha", "wa", None, None),
            P("section", None, "ha", "wa", None, None),
            P(None, "ha", "wa"),
        ),
        out_specs=P(None, "section", None, "ha", "wa", None, None),
        check_vma=False,
    )
```
